128 devices in a mesh: row: 16 (over z, y_hi, core), col: 8 (over y_lo, x).
Axes of the slice: x: 4, y: 4 (y_hi: 2, y_lo: 2; y = y_hi * 2 + y_lo), z: 4, core: 2. Of those that a mesh axis runs over, the one named last changes fastest.
Arguments:
- nodes: bfloat16 [32768, 512], P(('row', 'col')), may hold values from -6 to 6
- gain: float32 [512], replicated, may hold values from 0.1 to 1.9
- w_query: bfloat16 [512, 512], replicated
- w_key: bfloat16 [512, 512], replicated
- w_value: bfloat16 [512, 512], replicated, may hold values from -0.25 to 0.25
- w_out: bfloat16 [512, 512], replicated, may hold values from -0.75 to 0.75
- cotangent: bfloat16 [32768, 512], P(('row', 'col')), may hold values from -6 to 6
- tile_index: int32 [16, 8, 32, 2], P('row', 'col'), may hold values from 0 to 31, as said below
- tile_mask: int32 [16, 8, 32, 128, 128], P('row', 'col'), may hold values from 0 to 1, as said below
- tile_count: int32 [16, 8], P('row', 'col'), may hold values from 4 to 32, as said below
- node_order: int32 [32768], P(('row', 'col')), may hold values from 0 to 32767, as said below
Outputs:
- update: bfloat16 [32768, 512], P(('row', 'col'))
- node_grad: bfloat16 [32768, 512], P(('row', 'col'))
The draws below stay inside these ranges and needn't reach their ends.
Inputs may be any that keep to these rules, and one draw needn't show every extreme that they name: tile_index[i, j, t] = (r, s): r below 16, s below 32; the pairs of one cell are distinct; for t < 2 the pair is (j * 2 + t, i * 2 + t). `tile_mask`: the first 2 slots of every cell hold 1 on the diagonal. Slots of a cell at or after its tile_count are unused and hold arbitrary pairs and masks. `node_order`: a permutation of the 32768 nodes; the 256 owner rows of device p = i * 8 + j hold the nodes p * 256 to (p + 1) * 256 - 1 in some order.
All inputs are finite; a program needn't handle non-finite values.
Results may differ from the reference program's by a relative error of at most 0.022.
Values may be sent and summed in bfloat16 or wider, within the bound.
A program may use at most 128 MiB of HBM per device.

```python
import jax
import jax.numpy as jnp
from jax import lax

D = 512
HEADS = 4
HD = 128
TB = 128
NODE_DEV = 256
TILES = 32
NODES = 32768
RECV_ROWS = 2048
SEND_ROWS = 4096
N_ROW = 16
N_COL = 8


def shared_base(key):
    return jnp.clip(jax.random.normal(key, (D, D), jnp.float32), -4.0, 4.0) * D ** (-0.5)


def draw_w_query(key, part):
    key = jax.random.fold_in(key, 3)
    return shared_base(key).astype(jnp.bfloat16)


def draw_w_key(key, part):
    key = jax.random.fold_in(key, 4)
    return shared_base(key).astype(jnp.bfloat16)


def draw_tile_index(key, part):
    key = jax.random.fold_in(key, 5)
    recv_blocks = NODE_DEV * N_COL // TB
    send_blocks = NODE_DEV * N_ROW // TB
    own_blocks = NODE_DEV // TB
    tile_total = recv_blocks * send_blocks
    cell_count = N_ROW * N_COL
    cell_keys = jax.random.split(key, cell_count)
    cell_ids = jnp.arange(cell_count, dtype=jnp.int32)

    def one_cell(cell_key, cell_id):
        grid_row = cell_id // N_COL
        grid_col = cell_id % N_COL
        tile_ids = jax.random.permutation(cell_key, tile_total).astype(jnp.int32)
        recv_blk = tile_ids // send_blocks
        send_blk = tile_ids % send_blocks
        rel_recv = recv_blk - grid_col * own_blocks
        rel_send = send_blk - grid_row * own_blocks
        is_self = (rel_recv >= 0) & (rel_recv < own_blocks) & (rel_recv == rel_send)
        ranking = jnp.where(is_self, rel_recv, own_blocks).astype(jnp.int32)
        ordering = jnp.argsort(ranking, stable=True)
        chosen = tile_ids[ordering][:TILES]
        return jnp.stack([chosen // send_blocks, chosen % send_blocks], axis=1)
    tiles = jax.vmap(one_cell)(cell_keys, cell_ids)
    return tiles.reshape(N_ROW, N_COL, TILES, 2).astype(jnp.int32)


def draw_tile_mask(key, part):
    key = jax.random.fold_in(key, 7)
    draws = jax.random.randint(key, (N_ROW, N_COL, TILES, TB, TB), 0, 8)
    edges = draws == 0
    slot_ids = jnp.arange(TILES, dtype=jnp.int32)[:, None, None]
    diagonal = jnp.arange(TB)[:, None] == jnp.arange(TB)[None, :]
    edges = edges | (slot_ids < NODE_DEV // TB) & diagonal
    return edges.astype(jnp.int32)


def draw_tile_count(key, part):
    key = jax.random.fold_in(key, 9)
    first_key, second_key, third_key = jax.random.split(key, 3)
    cell_count = N_ROW * N_COL
    halving = jax.random.randint(first_key, (cell_count,), 0, 4)
    counts = TILES // jnp.left_shift(jnp.ones_like(halving), halving)
    busiest = jax.random.randint(second_key, (), 0, cell_count)
    lightest = (busiest + 1 + jax.random.randint(third_key, (), 0, cell_count - 1)) % cell_count
    cell_ids = jnp.arange(cell_count, dtype=jnp.int32)
    counts = jnp.where(cell_ids == busiest, TILES, jnp.where(cell_ids == lightest, TILES // 8, counts))
    return counts.reshape(N_ROW, N_COL).astype(jnp.int32)


def draw_node_order(key, part):
    key = jax.random.fold_in(key, 11)
    cell_count = N_ROW * N_COL
    cell_keys = jax.random.split(key, cell_count)
    local_order = jax.vmap(lambda cell_key: jax.random.permutation(cell_key, NODE_DEV))(cell_keys).astype(jnp.int32)
    offsets = jnp.arange(cell_count, dtype=jnp.int32)[:, None] * NODE_DEV
    return (offsets + local_order).reshape(-1).astype(jnp.int32)


def steps_of(stream_key, shape, cuts, low, largest):
    factor_of, own = 1.0, jax.random.fold_in(stream_key, 6)
    for position, parts in cuts:
        steps = jnp.exp(jax.random.uniform(jax.random.fold_in(own, position), (parts,), jnp.float32, low / len(cuts), largest / len(cuts)))
        factor_of = factor_of * jnp.repeat(steps, shape[position] // parts).reshape([-1 if axis == position else 1 for axis in range(len(shape))])
    return factor_of


def bell_draw(rng, extent, width, bound, shards=(), kind=jnp.bfloat16):
    level = steps_of(rng, extent, shards, -0.22, 0.18) if shards else 1.0
    values = jax.random.normal(rng, extent, jnp.float32) * width * level
    return jnp.minimum(jnp.maximum(values, -bound), bound).astype(kind)


def setup_inputs(seed: int = 0) -> dict:
    streams_of = jax.random.split(jax.random.key(seed), 12)
    nodes = bell_draw(streams_of[0], (NODES, D), 1.0, 6.0, ((0, 128),))
    gain = jnp.clip(1.0 + 0.18 * jax.random.normal(streams_of[1], (D,), jnp.float32), 0.1, 1.9)
    w_query = draw_w_query(jax.random.fold_in(streams_of[11], 71), 0)
    w_key = draw_w_key(jax.random.fold_in(streams_of[11], 71), 0)
    w_value = bell_draw(streams_of[4], (D, D), D ** -0.5, 0.25)
    w_out = bell_draw(streams_of[5], (D, D), (D // 8) ** -0.5, 0.75)
    cotangent = bell_draw(streams_of[6], (NODES, D), 1.0, 6.0, ((0, 128),))
    tile_index = draw_tile_index(jax.random.fold_in(streams_of[11], 71), 0)
    tile_mask = draw_tile_mask(jax.random.fold_in(streams_of[11], 71), 0)
    tile_count = draw_tile_count(jax.random.fold_in(streams_of[11], 71), 0)
    node_order = draw_node_order(jax.random.fold_in(streams_of[11], 71), 0)
    return {"nodes": nodes, "gain": gain, "w_query": w_query, "w_key": w_key, "w_value": w_value, "w_out": w_out, "cotangent": cotangent, "tile_index": tile_index, "tile_mask": tile_mask, "tile_count": tile_count, "node_order": node_order}


epsilon = 1e-05

def rounded(values):
    return lax.optimization_barrier(values.astype(jnp.bfloat16)).astype(jnp.float32)

def normalize(node_rows):
    values_f = node_rows.astype(jnp.float32)
    center = values_f - lax.optimization_barrier(jnp.mean(values_f, axis=1, keepdims=True))
    inv_std = lax.rsqrt(lax.optimization_barrier(jnp.mean(center * center, axis=1, keepdims=True)) + epsilon)
    return (center * inv_std, inv_std)

def cell_tiles(tile_index, tile_mask, tile_count, grid_row, grid_col):
    index_rows = tile_index[grid_row, grid_col]
    live_slot = jnp.arange(TILES, dtype=jnp.int32) < tile_count[grid_row, grid_col]
    edge_mask = (tile_mask[grid_row, grid_col] > 0) & live_slot[:, None, None]
    return (index_rows[:, 0], index_rows[:, 1], edge_mask)

def tile_scores(query_tile, key_tile, edge_mask):
    scores = jnp.einsum('ahd,bhd->hab', query_tile, key_tile) * HD ** (-0.5)
    return jnp.where(edge_mask[None], scores, -jnp.inf)

def reference(nodes, gain, w_query, w_key, w_value, w_out, cotangent, tile_index, tile_mask, tile_count, node_order):
    recv_blocks = RECV_ROWS // TB
    send_blocks = SEND_ROWS // TB
    grid_rows = jnp.arange(N_ROW, dtype=jnp.int32)
    grid_cols = jnp.arange(N_COL, dtype=jnp.int32)
    slot_ids = jnp.arange(TILES, dtype=jnp.int32)
    graph_nodes = jnp.zeros_like(nodes).at[node_order].set(nodes)
    unit_rows, inv_std = normalize(graph_nodes)
    normed = (unit_rows * gain).astype(jnp.bfloat16)
    query = jnp.dot(normed, w_query, preferred_element_type=jnp.float32).astype(jnp.bfloat16)
    key_proj = jnp.dot(normed, w_key, preferred_element_type=jnp.float32).astype(jnp.bfloat16)
    value_proj = jnp.dot(normed, w_value, preferred_element_type=jnp.float32).astype(jnp.bfloat16)

    def recv_layout(array):
        return array.astype(jnp.float32).reshape(N_ROW, recv_blocks, TB, HEADS, HD)

    def send_layout(array):
        moved = array.reshape(N_ROW, N_COL, NODE_DEV, D).transpose(1, 0, 2, 3)
        return moved.reshape(N_COL, send_blocks, TB, HEADS, HD).astype(jnp.float32)
    query_r = recv_layout(query)
    key_s = send_layout(key_proj)
    value_s = send_layout(value_proj)

    def cell_top(grid_row, grid_col):
        recv_idx, send_idx, edge_mask = cell_tiles(tile_index, tile_mask, tile_count, grid_row, grid_col)

        def step(row_top, slot_id):
            scores = tile_scores(query_r[grid_row, recv_idx[slot_id]], key_s[grid_col, send_idx[slot_id]], edge_mask[slot_id])
            return (row_top.at[recv_idx[slot_id]].max(lax.optimization_barrier(jnp.max(scores, axis=2))), None)
        start_top = jnp.full((recv_blocks, HEADS, TB), -jnp.inf, jnp.float32)
        return lax.scan(step, start_top, slot_ids)[0]

    def row_top_of(grid_row):
        return lax.optimization_barrier(jnp.max(lax.map(lambda grid_col: cell_top(grid_row, grid_col), grid_cols), axis=0))
    row_top = lax.map(row_top_of, grid_rows)

    def row_sums(grid_row):

        def cell(carried, grid_col):
            recv_idx, send_idx, edge_mask = cell_tiles(tile_index, tile_mask, tile_count, grid_row, grid_col)

            def step(state, slot_id):
                weighted, totals = state
                recv_blk = recv_idx[slot_id]
                send_blk = send_idx[slot_id]
                scores = tile_scores(query_r[grid_row, recv_blk], key_s[grid_col, send_blk], edge_mask[slot_id])
                weight = jnp.exp(scores - row_top[grid_row, recv_blk][:, :, None])
                totals = totals.at[recv_blk].add(lax.optimization_barrier(jnp.sum(weight, axis=2)))
                weighted = weighted.at[recv_blk].add(jnp.einsum('hab,bhd->ahd', rounded(weight), value_s[grid_col, send_blk]))
                return ((weighted, totals), None)
            return (lax.scan(step, carried, slot_ids)[0], None)
        start = (jnp.zeros((recv_blocks, TB, HEADS, HD), jnp.float32), jnp.zeros((recv_blocks, HEADS, TB), jnp.float32))
        return lax.scan(cell, start, grid_cols)[0]
    weighted, totals = lax.map(row_sums, grid_rows)
    attended = (weighted / jnp.swapaxes(totals, 2, 3)[..., None]).reshape(NODES, D).astype(jnp.bfloat16)
    update_graph = jnp.dot(attended, w_out, preferred_element_type=jnp.float32).astype(jnp.bfloat16)
    graph_grad = jnp.zeros_like(cotangent).at[node_order].set(cotangent)
    d_attn = jnp.dot(graph_grad, w_out.T, preferred_element_type=jnp.float32).astype(jnp.bfloat16)
    product = d_attn.astype(jnp.float32) * attended.astype(jnp.float32)
    deltas = lax.optimization_barrier(jnp.sum(product.reshape(N_ROW, recv_blocks, TB, HEADS, HD), axis=4)).transpose(0, 1, 3, 2)
    grad_r = recv_layout(d_attn)

    def row_grads(carried, grid_row):

        def cell(state, grid_col):
            query_acc, key_all, value_all = state
            recv_idx, send_idx, edge_mask = cell_tiles(tile_index, tile_mask, tile_count, grid_row, grid_col)

            def step(inner, slot_id):
                query_part, key_part, value_part = inner
                recv_blk = recv_idx[slot_id]
                send_blk = send_idx[slot_id]
                query_tile = query_r[grid_row, recv_blk]
                key_tile = key_s[grid_col, send_blk]
                value_tile = value_s[grid_col, send_blk]
                grad_tile = grad_r[grid_row, recv_blk]
                scores = tile_scores(query_tile, key_tile, edge_mask[slot_id])
                norm_weight = jnp.exp(scores - row_top[grid_row, recv_blk][:, :, None]) / totals[grid_row, recv_blk][:, :, None]
                d_prob = jnp.einsum('ahd,bhd->hab', grad_tile, value_tile)
                d_score = rounded(norm_weight * (d_prob - deltas[grid_row, recv_blk][:, :, None]) * HD ** (-0.5))
                query_part = query_part.at[recv_blk].add(jnp.einsum('hab,bhd->ahd', d_score, key_tile))
                key_part = key_part.at[send_blk].add(jnp.einsum('hab,ahd->bhd', d_score, query_tile))
                value_part = value_part.at[send_blk].add(jnp.einsum('hab,ahd->bhd', rounded(norm_weight), grad_tile))
                return ((query_part, key_part, value_part), None)
            zero_send = jnp.zeros((send_blocks, TB, HEADS, HD), jnp.float32)
            (query_acc, key_cell, value_cell), _ = lax.scan(step, (query_acc, zero_send, zero_send), slot_ids)
            return ((query_acc, key_all.at[grid_col].add(key_cell), value_all.at[grid_col].add(value_cell)), None)
        key_all, value_all = carried
        zero_recv = jnp.zeros((recv_blocks, TB, HEADS, HD), jnp.float32)
        (query_acc, key_all, value_all), _ = lax.scan(cell, (zero_recv, key_all, value_all), grid_cols)
        return ((key_all, value_all), query_acc)
    zero_all = jnp.zeros((N_COL, send_blocks, TB, HEADS, HD), jnp.float32)
    (key_all, value_all), query_acc = lax.scan(row_grads, (zero_all, zero_all), grid_rows)

    def graph_layout(array):
        return array.reshape(N_COL, N_ROW, NODE_DEV, D).transpose(1, 0, 2, 3).reshape(NODES, D)
    d_query = query_acc.reshape(NODES, D)
    d_key = graph_layout(key_all)
    d_value = graph_layout(value_all)
    exact = lax.Precision.HIGHEST
    d_normed = jnp.dot(d_query, w_query.astype(jnp.float32).T, precision=exact)
    d_normed = d_normed + jnp.dot(d_key, w_key.astype(jnp.float32).T, precision=exact)
    d_normed = d_normed + jnp.dot(d_value, w_value.astype(jnp.float32).T, precision=exact)
    scaled = d_normed * gain
    grad_graph = inv_std * (scaled - lax.optimization_barrier(jnp.mean(scaled, axis=1, keepdims=True)) - unit_rows * lax.optimization_barrier(jnp.mean(scaled * unit_rows, axis=1, keepdims=True)))
    return (update_graph[node_order], grad_graph.astype(jnp.bfloat16)[node_order])
```

```python
import jax
import jax.numpy as jnp
from jax import lax
from jax.experimental import pallas as pl
from jax.experimental.pallas import tpu as pltpu
from jax.sharding import PartitionSpec as P

HEADS = 4
HD = 128
D = 512
TB = 128
OWN = 256
TILES = 32
RB = 16
SB = 32
EPS = 1e-05
LOG2E = 1.4426950408889634
SCALE = HD ** (-0.5)
FLOOR = -3.4028235e38
MESH = pl.DeviceIdType.MESH
F32 = jnp.float32
BF16 = jnp.bfloat16
SEMS = 256
UNROLL = 4


def mm(a, b):
    return jnp.dot(a, b, preferred_element_type=F32)


def mm_nt(a, b):
    return lax.dot_general(a, b, (((1,), (1,)), ((), ())), preferred_element_type=F32)


def mm_tn(a, b):
    return lax.dot_general(a, b, (((0,), (0,)), ((), ())), preferred_element_type=F32)


def body(
    meta,
    order,
    rcol,
    nodes,
    cot,
    gain,
    wq,
    wk,
    wv,
    wo,
    mask,
    out_update,
    out_grad,
    perm_s,
    unit_s,
    inv_s,
    nall,
    qd0,
    qd1,
    qd2,
    qd3,
    kv,
    bias,
    wgt,
    dpr,
    m_s,
    l_s,
    d_s,
    p_s,
    ds_s,
    acc1,
    acc2,
    od,
    ra,
    rb,
    rd,
    fin,
    dkv,
    pd,
    pa,
    pb,
    pe,
    st_send,
    st_recv,
    gs0,
    gs1,
    gs2,
    gs3,
    ss,
    rs,
):
    qd = [qd0, qd1, qd2, qd3]
    gstat = [gs0, gs1, gs2, gs3]
    i = lax.axis_index("row")
    j = lax.axis_index("col")
    z, yh, c = i // 4, (i // 2) % 2, i % 2
    yl, x = j // 4, j % 4

    def row_id(z_, yh_, c_):
        return (z_ * 2 + yh_) * 2 + c_

    def col_id(yl_, x_):
        return yl_ * 4 + x_

    zp, zm, zo = (z + 1) % 4, (z + 3) % 4, (z + 2) % 4
    xp, xm, xo = (x + 1) % 4, (x + 3) % 4, (x + 2) % 4
    oh, ol, oc = 1 - yh, 1 - yl, 1 - c
    sib = (row_id(z, yh, oc), j)
    yhp = (row_id(z, oh, c), j)
    dzp = (row_id(zp, yh, c), j)
    dzm = (row_id(zm, yh, c), j)
    ylp = (i, col_id(ol, x))
    dxp = (i, col_id(yl, xp))
    dxm = (i, col_id(yl, xm))

    made = []

    def copy(src, dst, dev):
        k = len(made)
        d = pltpu.make_async_remote_copy(
            src_ref=src,
            dst_ref=dst,
            send_sem=ss.at[k],
            recv_sem=rs.at[k],
            device_id=dev,
            device_id_type=MESH,
        )
        made.append(d)
        d.start()
        return d

    peers = [(i, lax.rem(j + k, 8)) for k in range(1, 8)]
    barrier = pltpu.get_barrier_semaphore()
    for dev in [sib, yhp, dzp, dzm] + peers:
        pl.semaphore_signal(barrier, inc=1, device_id=dev, device_id_type=MESH)

    perm = jnp.where(
        lax.broadcasted_iota(jnp.int32, (OWN, OWN), 0) == order[...], 1.0, 0.0
    ).astype(BF16)
    perm_s[...] = perm
    rows = mm(perm, nodes[...])
    center = rows - jnp.mean(rows, axis=1, keepdims=True)
    inv = lax.rsqrt(jnp.mean(center * center, axis=1, keepdims=True) + EPS)
    unit = center * inv
    unit_s[...] = unit
    inv_s[...] = jnp.broadcast_to(inv, (OWN, 128))
    normed = (unit * gain[...]).astype(BF16)
    own = row_id(z, yh, c)
    nall[own] = normed
    query = mm(normed, wq[...]).astype(BF16)
    grads = mm_nt(mm(perm, cot[...]).astype(BF16), wo[...]).astype(BF16)
    for h in range(HEADS):
        cols = slice(h * HD, (h + 1) * HD)
        for a in range(2):
            qd[h][2 * j + a, 0] = query[a * TB : (a + 1) * TB, cols]
            qd[h][2 * j + a, 1] = grads[a * TB : (a + 1) * TB, cols]

    pl.semaphore_wait(barrier, 11)

    def nsend(b, dev):
        return copy(nall.at[b], nall.at[b], dev)

    def nhalf(b, half, dev):
        part = nall.at[b, pl.ds(half * TB, TB)]
        return copy(part, part, dev)

    def qsend(h, b, dev):
        part = qd[h].at[pl.ds(2 * b, 2)]
        return copy(part, part, dev)

    def qhalf(h, b, half, dev):
        part = qd[h].at[2 * b + half]
        return copy(part, part, dev)

    n_y = nsend(own, yhp)
    n_p = nsend(own, dzp)
    n_m = nsend(own, dzm)
    sibs = [nsend(own, sib)]
    cy, cp, cm = [], [], []
    for h in range(HEADS):
        cy.append(qsend(h, j, ylp))
        cp.append(qsend(h, j, dxp))
        cm.append(qsend(h, j, dxm))

    def project(b):
        rows = nall[b]
        k_rows = mm(rows, wk[...]).astype(BF16)
        v_rows = mm(rows, wv[...]).astype(BF16)
        for h in range(HEADS):
            cols = slice(h * HD, (h + 1) * HD)
            for a in range(2):
                kv[h, 2 * b + a, 0] = k_rows[a * TB : (a + 1) * TB, cols]
                kv[h, 2 * b + a, 1] = v_rows[a * TB : (a + 1) * TB, cols]

    def make_bias(t, carry):
        tile = mask[meta[2, t]].astype(F32)
        bias[t] = jnp.where(tile.T > meta[4, t].astype(F32), 0.0, -jnp.inf)
        return carry

    lax.fori_loop(0, TILES // 2, make_bias, 0)
    yb = row_id(z, oh, c)
    n_y.wait_recv()
    ny_p = nsend(yb, dzp)
    ny_m = nsend(yb, dzm)
    sibs.append(nsend(yb, sib))
    cyp, cym = [], []
    for h in range(HEADS):
        cy[h].wait_recv()
        b = col_id(ol, x)
        cyp.append(qsend(h, b, dxp))
        cym.append(qsend(h, b, dxm))
    lax.fori_loop(TILES // 2, TILES, make_bias, 0)
    project(own)
    project(yb)

    far = []
    for got_p, got_m, h_ in ((n_p, n_m, yh), (ny_p, ny_m, oh)):
        got_p.wait_recv()
        b = row_id(zm, h_, c)
        far.append(nhalf(b, 0, dzp))
        sibs.append(nsend(b, sib))
        project(b)
        got_m.wait_recv()
        b = row_id(zp, h_, c)
        far.append(nhalf(b, 1, dzm))
        sibs.append(nsend(b, sib))
        project(b)

    qfar = []
    for h in range(HEADS):
        for got_p, got_m, l_ in ((cp, cm, yl), (cyp, cym, ol)):
            got_p[h].wait_recv()
            qfar.append(qhalf(h, col_id(l_, xm), 0, dxp))
            got_m[h].wait_recv()
            qfar.append(qhalf(h, col_id(l_, xp), 1, dxm))

    for n, h_ in ((0, yh), (2, oh)):
        b = row_id(zo, h_, c)
        for half in range(2):
            far[n + half].wait_recv()
            sibs.append(nhalf(b, half, sib))
        project(b)
    for d in sibs:
        d.wait_recv()

    def project_other(k, carry):
        project(2 * k + oc)
        return carry

    lax.fori_loop(0, 8, project_other, 0)
    for d in qfar:
        d.wait_recv()

    def forward(h, first, last):
        slot = h % 2

        def step(g, carry):
            for u in range(UNROLL):
                t = g * UNROLL + u
                r, s = meta[0, t], meta[1, t]
                scores = mm_nt(kv[h, s, 0], qd[h][r, 0]) * (SCALE * LOG2E) + bias[t]
                top = jnp.maximum(jnp.max(scores, axis=0, keepdims=True), FLOOR)
                w = jnp.exp2(scores - top)
                dp = mm_nt(kv[h, s, 1], qd[h][r, 1])
                wgt[slot, t] = w
                dpr[slot, t] = dp
                m_s[h, pl.ds(t, 1), :] = top
                l_s[h, pl.ds(t, 1), :] = jnp.sum(w, axis=0, keepdims=True)
                d_s[h, pl.ds(t, 1), :] = jnp.sum(w * dp, axis=0, keepdims=True)
            return carry

        lax.fori_loop(first // UNROLL, last // UNROLL, step, 0)

    def stat_send(h):
        r_of = rcol[...]
        tops, sums, dots = m_s[h], l_s[h], d_s[h]
        for r in range(RB):
            here = r_of == r
            top = jnp.max(jnp.where(here, tops, FLOOR), axis=0, keepdims=True)
            scale = jnp.where(here, jnp.exp2(tops - top), 0.0)
            owner, a = r // 2, r % 2
            st_send[h, owner, a : a + 1, :] = top
            st_send[h, owner, 2 + a : 3 + a, :] = jnp.sum(scale * sums, axis=0, keepdims=True)
            st_send[h, owner, 4 + a : 5 + a, :] = jnp.sum(scale * dots, axis=0, keepdims=True)
        st_recv[h, j] = st_send[h, j]
        return [copy(st_send.at[h, peer[1]], st_recv.at[h, j], peer) for peer in peers]

    def stat_merge(h, sent):
        for d in sent:
            d.wait_recv()
        tops = [st_recv[h, k, 0:2, :] for k in range(8)]
        top = tops[0]
        for k in range(1, 8):
            top = jnp.maximum(top, tops[k])
        total = jnp.zeros((2, 128), F32)
        dot = jnp.zeros((2, 128), F32)
        for k in range(8):
            scale = jnp.exp2(tops[k] - top)
            total = total + scale * st_recv[h, k, 2:4, :]
            dot = dot + scale * st_recv[h, k, 4:6, :]
        gstat[h][j, 0:2, :] = top
        gstat[h][j, 2:4, :] = 1.0 / total
        gstat[h][j, 4:6, :] = dot / total
        return [copy(gstat[h].at[j], gstat[h].at[j], peer) for peer in peers]

    def stat_wait(sent):
        for d in sent:
            d.wait_recv()

    def backward_recv(h):
        slot = h % 2
        acc1[0] = jnp.zeros((TB, HD), F32)
        acc2[0] = jnp.zeros((TB, HD), F32)

        def step(g, carry):
            for u in range(UNROLL):
                t = g * UNROLL + u
                r, s = meta[0, t], meta[1, t]
                owner, a = r // 2, r % 2
                top = gstat[h][owner, pl.ds(a, 1), :]
                inv_total = gstat[h][owner, pl.ds(2 + a, 1), :]
                delta = gstat[h][owner, pl.ds(4 + a, 1), :]
                fix = jnp.exp2(m_s[h, pl.ds(t, 1), :] - top) * inv_total
                prob = wgt[slot, t] * fix
                dscore = prob * (dpr[slot, t] - delta) * SCALE
                prob = prob.astype(BF16)
                dscore = dscore.astype(BF16)
                p_s[t] = prob
                ds_s[t] = dscore
                same = meta[3, t] > 0
                acc1[t + 1] = jnp.where(same, acc1[t], 0.0) + mm_tn(prob, kv[h, s, 1])
                acc2[t + 1] = jnp.where(same, acc2[t], 0.0) + mm_tn(dscore, kv[h, s, 0])
            return carry

        lax.fori_loop(0, TILES // UNROLL, step, 0)
        for r in range(RB):
            at = meta[7, r]
            od[h, r, 0] = acc1[at].astype(BF16)
            od[h, r, 1] = acc2[at].astype(BF16)

    def backward_send(h):
        def step(g, carry):
            for u in range(UNROLL):
                n = g * UNROLL + u
                t, r = meta[5, n], meta[9, n]
                same = meta[6, n] > 0
                acc1[n + 1] = jnp.where(same, acc1[n], 0.0) + mm(ds_s[t], qd[h][r, 0])
                acc2[n + 1] = jnp.where(same, acc2[n], 0.0) + mm(p_s[t], qd[h][r, 1])
            return carry

        lax.fori_loop(0, TILES // UNROLL, step, 0)
        for s in range(SB):
            at = meta[8, s]
            dkv[s, :, h * HD : (h + 1) * HD] = acc1[at].astype(BF16)
            dkv[s, :, D + h * HD : D + (h + 1) * HD] = acc2[at].astype(BF16)

    def osend_a(h):
        sent = []
        for l_ in range(2):
            b = col_id(l_, xo)
            sent.append(copy(od.at[h, 2 * b], ra.at[h, 0, l_], dxp))
            sent.append(copy(od.at[h, 2 * b + 1], ra.at[h, 1, l_], dxm))
        return sent

    def osend_b(h, sent):
        for d in sent:
            d.wait_recv()
        out = []
        for l_ in range(2):
            b = col_id(l_, xp)
            od[h, 2 * b] = (od[h, 2 * b].astype(F32) + ra[h, 0, l_].astype(F32)).astype(BF16)
            out.append(copy(od.at[h, pl.ds(2 * b, 2)], rb.at[h, 0, l_], dxp))
            b = col_id(l_, xm)
            od[h, 2 * b + 1] = (od[h, 2 * b + 1].astype(F32) + ra[h, 1, l_].astype(F32)).astype(BF16)
            out.append(copy(od.at[h, pl.ds(2 * b, 2)], rb.at[h, 1, l_], dxm))
        return out

    def osend_d(h, sent):
        for d in sent:
            d.wait_recv()
        for l_ in (ol, yl):
            b = col_id(l_, x)
            for a in range(2):
                od[h, 2 * b + a] = (
                    od[h, 2 * b + a].astype(F32)
                    + rb[h, 0, l_, a].astype(F32)
                    + rb[h, 1, l_, a].astype(F32)
                ).astype(BF16)
        return copy(od.at[h, pl.ds(2 * col_id(ol, x), 2)], rd.at[h], ylp)

    def ofinish(h, sent):
        sent.wait_recv()
        for a in range(2):
            for k in range(2):
                fin[k, a * TB : (a + 1) * TB, h * HD : (h + 1) * HD] = (
                    od[h, 2 * j + a, k].astype(F32) + rd[h, a, k].astype(F32)
                ).astype(BF16)

    forward(0, 0, TILES)
    s0 = stat_send(0)
    forward(1, 0, TILES // 2)
    g0 = stat_merge(0, s0)
    forward(1, TILES // 2, TILES)
    s1 = stat_send(1)
    stat_wait(g0)
    backward_recv(0)
    a0 = osend_a(0)
    g1 = stat_merge(1, s1)
    backward_send(0)
    b0 = osend_b(0, a0)
    forward(2, 0, TILES)
    s2 = stat_send(2)
    d0 = osend_d(0, b0)
    stat_wait(g1)
    backward_recv(1)
    a1 = osend_a(1)
    g2 = stat_merge(2, s2)
    backward_send(1)
    b1 = osend_b(1, a1)
    ofinish(0, d0)
    forward(3, 0, TILES)
    s3 = stat_send(3)
    d1 = osend_d(1, b1)
    stat_wait(g2)
    backward_recv(2)
    a2 = osend_a(2)
    g3 = stat_merge(3, s3)
    backward_send(2)
    b2 = osend_b(2, a2)
    ofinish(1, d1)
    stat_wait(g3)
    backward_recv(3)
    a3 = osend_a(3)
    d2 = osend_d(2, b2)
    backward_send(3)
    b3 = osend_b(3, a3)

    for d in [n_y, n_p, n_m, ny_p, ny_m] + sibs + far:
        d.wait_send()

    def pair_back(b):
        pair = dkv[pl.ds(2 * b, 2)].reshape(OWN, 2 * D)
        nall[b] = (mm_nt(pair[:, :D], wk[...]) + mm_nt(pair[:, D:], wv[...])).astype(BF16)

    tosib = []
    for n, z_ in enumerate((zo, zp, zm, z)):
        for h_ in range(2):
            b = row_id(z_, h_, oc)
            pair_back(b)
            tosib.append(copy(nall.at[b], pd.at[n, h_], sib))
    for z_ in (zo, zp, zm, z):
        for h_ in range(2):
            pair_back(row_id(z_, h_, c))
    d3 = osend_d(3, b3)
    ofinish(2, d2)

    def merge_sib(n, z_, h_):
        tosib[2 * n + h_].wait_recv()
        b = row_id(z_, h_, c)
        nall[b] = (nall[b].astype(F32) + pd[n, h_].astype(F32)).astype(BF16)

    pa_sent = []
    for h_ in range(2):
        merge_sib(0, zo, h_)
        b = row_id(zo, h_, c)
        pa_sent.append(copy(nall.at[b, pl.ds(0, TB)], pa.at[0, h_], dzp))
        pa_sent.append(copy(nall.at[b, pl.ds(TB, TB)], pa.at[1, h_], dzm))
    for h_ in range(2):
        merge_sib(1, zp, h_)
        merge_sib(2, zm, h_)
        merge_sib(3, z, h_)
    pb_sent = []
    for h_ in range(2):
        for side, z_, dev in ((0, zp, dzp), (1, zm, dzm)):
            pa_sent[2 * h_ + side].wait_recv()
            b = row_id(z_, h_, c)
            part = slice(side * TB, (side + 1) * TB)
            nall[b, part, :] = (
                nall[b, part, :].astype(F32) + pa[side, h_].astype(F32)
            ).astype(BF16)
            pb_sent.append(copy(nall.at[b], pb.at[side, h_], dev))
    ofinish(3, d3)

    update = mm(fin[0], wo[...]).astype(BF16)
    out_update[...] = mm_tn(perm_s[...], update).astype(BF16)
    d_normed = mm_nt(fin[1], wq[...])

    for d in pb_sent:
        d.wait_recv()

    def z_sum(h_):
        return (
            nall[row_id(z, h_, c)].astype(F32)
            + pb[0, h_].astype(F32)
            + pb[1, h_].astype(F32)
        )

    nall[row_id(z, oh, c)] = z_sum(oh).astype(BF16)
    pe_sent = copy(nall.at[row_id(z, oh, c)], pe, yhp)
    d_normed = d_normed + z_sum(yh)
    pe_sent.wait_recv()
    d_normed = d_normed + pe[...].astype(F32)
    scaled = d_normed * gain[...]
    unit = unit_s[...]
    grad = inv_s[:, 0:1] * (
        scaled
        - jnp.mean(scaled, axis=1, keepdims=True)
        - unit * jnp.mean(scaled * unit, axis=1, keepdims=True)
    )
    out_grad[...] = mm_tn(perm_s[...], grad.astype(BF16)).astype(BF16)

    waited = [n_y, n_p, n_m, ny_p, ny_m] + sibs + far
    for d in made:
        if not any(d is w for w in waited):
            d.wait_send()


def order_lists(tile_index, tile_count):
    slots = jnp.arange(TILES, dtype=jnp.int32)
    live = slots < tile_count
    r = jnp.clip(tile_index[:, 0], 0, RB - 1)
    s = jnp.clip(tile_index[:, 1], 0, SB - 1)

    def sort_places(key):
        whole = key * TILES + slots
        rank = jnp.sum((whole[:, None] > whole[None, :]).astype(jnp.int32), axis=1)
        return (rank[None, :] == slots[:, None]).astype(jnp.int32)

    def take(pick, values):
        return jnp.sum(pick * values[None, :], axis=1)

    def same_as_before(key):
        return jnp.concatenate([jnp.zeros((1,), jnp.int32), (key[1:] == key[:-1]).astype(jnp.int32)])

    def last_of(key, count):
        blocks = jnp.arange(TILES, dtype=jnp.int32)
        hit = key[None, :] == blocks[:, None]
        return jnp.max(jnp.where(hit, slots[None, :] + 1, 0), axis=1)

    by_r = sort_places(r)
    r1, s1 = take(by_r, r), take(by_r, s)
    slot1 = take(by_r, slots)
    limit = jnp.where(take(by_r, live.astype(jnp.int32)) > 0, 0, 2)
    by_s = sort_places(s1)
    place2 = take(by_s, slots)
    r2, s2 = take(by_s, r1), take(by_s, s1)
    meta = jnp.stack(
        [
            r1,
            s1,
            slot1,
            same_as_before(r1),
            limit,
            place2,
            same_as_before(s2),
            last_of(r1, RB),
            last_of(s2, SB),
            r2,
        ]
    )
    return meta, jnp.broadcast_to(r1[:, None], (TILES, 128))


def local(
    nodes,
    gain,
    w_query,
    w_key,
    w_value,
    w_out,
    cotangent,
    tile_index,
    tile_mask,
    tile_count,
    node_order,
):
    meta, rcol = order_lists(tile_index[0, 0], tile_count[0, 0])
    order = (node_order % OWN).reshape(1, OWN)
    vmem = pl.BlockSpec(memory_space=pltpu.VMEM)
    smem = pl.BlockSpec(memory_space=pltpu.SMEM)
    out = jax.ShapeDtypeStruct((OWN, D), BF16)
    return pl.pallas_call(
        body,
        out_shape=(out, out),
        in_specs=[smem] + [vmem] * 10,
        out_specs=(vmem, vmem),
        scratch_shapes=[
            pltpu.VMEM((OWN, OWN), BF16),
            pltpu.VMEM((OWN, D), F32),
            pltpu.VMEM((OWN, 128), F32),
            pltpu.VMEM((16, OWN, D), BF16),
            *[pltpu.VMEM((RB, 2, TB, HD), BF16)] * HEADS,
            pltpu.VMEM((HEADS, SB, 2, TB, HD), BF16),
            pltpu.VMEM((TILES, TB, TB), F32),
            pltpu.VMEM((2, TILES, TB, TB), F32),
            pltpu.VMEM((2, TILES, TB, TB), F32),
            pltpu.VMEM((HEADS, TILES, 128), F32),
            pltpu.VMEM((HEADS, TILES, 128), F32),
            pltpu.VMEM((HEADS, TILES, 128), F32),
            pltpu.VMEM((TILES, TB, TB), BF16),
            pltpu.VMEM((TILES, TB, TB), BF16),
            pltpu.VMEM((TILES + 1, TB, HD), F32),
            pltpu.VMEM((TILES + 1, TB, HD), F32),
            pltpu.VMEM((HEADS, RB, 2, TB, HD), BF16),
            pltpu.VMEM((HEADS, 2, 2, 2, TB, HD), BF16),
            pltpu.VMEM((HEADS, 2, 2, 2, 2, TB, HD), BF16),
            pltpu.VMEM((HEADS, 2, 2, TB, HD), BF16),
            pltpu.VMEM((2, OWN, D), BF16),
            pltpu.VMEM((SB, TB, 2 * D), BF16),
            pltpu.VMEM((4, 2, OWN, D), BF16),
            pltpu.VMEM((2, 2, TB, D), BF16),
            pltpu.VMEM((2, 2, OWN, D), BF16),
            pltpu.VMEM((OWN, D), BF16),
            pltpu.VMEM((HEADS, 8, 8, 128), F32),
            pltpu.VMEM((HEADS, 8, 8, 128), F32),
            *[pltpu.VMEM((8, 8, 128), F32)] * HEADS,
            pltpu.SemaphoreType.DMA((SEMS,)),
            pltpu.SemaphoreType.DMA((SEMS,)),
        ],
        compiler_params=pltpu.CompilerParams(
            collective_id=0,
            has_side_effects=True,
            vmem_limit_bytes=63 * 1024 * 1024,
        ),
        cost_estimate=pl.CostEstimate(
            flops=13_000_000_000, bytes_accessed=8_000_000, transcendentals=2_100_000
        ),
    )(
        meta,
        order,
        rcol,
        nodes,
        cotangent,
        gain.reshape(1, D),
        w_query,
        w_key,
        w_value,
        w_out,
        tile_mask[0, 0],
    )


def solution(mesh):
    placed = (
        P(("row", "col"), None),
        P(),
        P(),
        P(),
        P(),
        P(),
        P(("row", "col"), None),
        P("row", "col", None, None),
        P("row", "col", None, None, None),
        P("row", "col"),
        P(("row", "col")),
    )
    return jax.shard_map(
        local,
        mesh=mesh,
        in_specs=placed,
        out_specs=(P(("row", "col"), None), P(("row", "col"), None)),
        check_vma=False,
    )
```
